32 devices in a mesh: groups: 2 (over x), blk: 16 (over z, y, core).
Axes of the slice: x: 2, y: 2, z: 4, core: 2. Of those that a mesh axis runs over, the one named last changes fastest.
Arguments:
- wavefunction: bfloat16 [384, 128, 128], P(('groups', 'blk')), parts along dimension 0, may hold values from -6 to 6
- left_blocks: bfloat16 [7680, 128, 128], P(('groups', 'blk')), parts along dimension 0, may hold values from -0.5 to 0.5
- right_blocks: bfloat16 [2560, 128, 128], P(('groups', 'blk')), parts along dimension 0, may hold values from -0.078125 to 0.078125
- right_env: int32 [64, 40], P(('groups', 'blk')), parts along dimension 0, may hold values from 0 to 1279, as said below
- pair_sectors: int32 [384, 2], P(('groups', 'blk')), parts along dimension 0, may hold values from 0 to 5, as said below
- channel_mask: int32 [384, 40], P(('groups', 'blk')), parts along dimension 0, may hold values 0 or 1
Outputs:
- applied_state: float32 [384, 128, 128], P(('groups', 'blk')), parts along dimension 0
The draws below stay inside these ranges and needn't reach their ends.
There are 2 independent parts, one for each index of `groups`. The reference program is written for one: setup_inputs(seed, part) draws one part's arguments, and reference() takes and returns one part's arrays. A program takes and returns all parts, laid end to end along the dimension named above; each array names one. Nothing has to cross between parts.
Inputs may be any that keep to these rules, and one draw needn't show every extreme that they name: `right_env`: the 80 entries of one device are distinct; among them no owner device (entry // 80) is named more than 8 times, and some owner exactly 8 times. Devices may name the same blocks. `pair_sectors`: on each device the pairs list every combination of a left sector index below 6 and a right sector index below 2 exactly once.
All inputs are finite; a program needn't handle non-finite values. No bound on the sum of `channel_mask` on one device may be relied on, other than what follows from the above.
Results may differ from the reference program's by a relative error of at most 0.0041.
Values may be sent and summed in bfloat16 or wider, within the bound.
A program may use at most 128 MiB of HBM per device.

```python
import jax
import jax.numpy as jnp
from jax import lax

B = 128
A = 40
LSEC = 6
RUSE = 2
NP = 192
LEFTS = 3840
ENVS = 1280
CAP = 8
N_BLK = 16


def draw_right_env(key, part):
    key = jax.random.fold_in(key, 11)
    count = RUSE * A
    stored = RUSE * A
    key_hot, key_rest, key_order, key_offset = jax.random.split(key, 4)
    hottest = jax.random.randint(key_hot, (N_BLK,), 0, N_BLK)
    shuffled = jax.vmap(lambda k: jax.random.permutation(k, (N_BLK - 1) * CAP))(jax.random.split(key_rest, N_BLK))
    others = shuffled[:, :count - CAP] // CAP
    others = jnp.where(others >= hottest[:, None], others + 1, others)
    owners = jnp.concatenate([jnp.broadcast_to(hottest[:, None], (N_BLK, CAP)), others], axis=1)
    order = jax.vmap(lambda k: jax.random.permutation(k, count))(jax.random.split(key_order, N_BLK))
    owners = jnp.take_along_axis(owners, order, axis=1)
    onehot = (owners[:, :, None] == jnp.arange(N_BLK, dtype=jnp.int32)[None, None, :]).astype(jnp.int32)
    ranks = jnp.sum(jnp.cumsum(onehot, axis=1) * onehot, axis=2) - 1
    offsets = jax.random.randint(key_offset, (N_BLK, N_BLK), 0, stored)
    starts = jnp.take_along_axis(offsets, owners, axis=1)
    local_ids = (starts + ranks) % stored
    block_ids = owners * stored + local_ids
    return block_ids.reshape(N_BLK * RUSE, A).astype(jnp.int32)


def draw_pair_sectors(key, part):
    key = jax.random.fold_in(key, 5)
    per_device = LSEC * RUSE
    order = jax.vmap(lambda k: jax.random.permutation(k, per_device))(jax.random.split(key, N_BLK))
    combos = order.reshape(N_BLK * per_device)
    return jnp.stack([combos // RUSE, combos % RUSE], axis=1).astype(jnp.int32)


def with_ends(values, key, smallest, largest):
    index_at = [jax.random.randint(jax.random.fold_in(key, axis), (), 0, length) for axis, length in enumerate(values.shape)]
    widest = values.shape.index(max(values.shape))
    neighbour = index_at[:widest] + [(index_at[widest] + 1) % values.shape[widest]] + index_at[widest + 1:]
    return values.at[tuple(index_at)].set(smallest).at[tuple(neighbour)].set(largest)


def levels(rng, dims, cuts, low, high):
    def one(dim, shards_of):
        heights = jax.random.uniform(jax.random.fold_in(jax.random.fold_in(rng, 6), dim), (shards_of,), jnp.float32, low / len(cuts), high / len(cuts))
        return jnp.repeat(jnp.exp(heights), dims[dim] // shards_of).reshape((-1,) + (1,) * (len(dims) - dim - 1))

    gain = one(*cuts[0])
    for cut in cuts[1:]:
        gain = gain * one(*cut)
    return gain


def bell_draw(own_key, dims, width, limit, cuts=(), held_as=jnp.bfloat16):
    drawn = width * jax.random.normal(own_key, dims, jnp.float32)
    if cuts:
        drawn = drawn * levels(own_key, dims, cuts, -0.22, 0.18)
    return jnp.clip(drawn, -limit, limit).astype(held_as)


def setup_inputs(seed: int = 0, part: int = 0) -> dict:
    key_list = jax.random.split(jax.random.key(seed), 7)
    part_keys = jax.random.split(jax.random.fold_in(key_list[6], part), 7)
    return {
        "wavefunction": bell_draw(part_keys[0], (NP, B, B), 1.0, 6.0, ((0, 16),)),
        "left_blocks": bell_draw(part_keys[1], (LEFTS, B, B), B ** -0.5, 0.5, ((0, 16),)),
        "right_blocks": bell_draw(part_keys[2], (ENVS, B, B), (B * A) ** -0.5, 0.078125, ((0, 16),)),
        "right_env": draw_right_env(jax.random.fold_in(jax.random.fold_in(key_list[6], part), 71), part),
        "pair_sectors": draw_pair_sectors(jax.random.fold_in(jax.random.fold_in(key_list[6], part), 71), part),
        "channel_mask": with_ends((jax.random.randint(part_keys[5], (NP, A), 0, 4) < 3).astype(jnp.int32), jax.random.fold_in(part_keys[5], 1), 0, 1),
    }


def reference(wavefunction, left_blocks, right_blocks, right_env, pair_sectors, channel_mask):
    per_device = LSEC * RUSE

    def one_pair(index):
        source = index // per_device
        left_sector = source * LSEC + pair_sectors[index, 0]
        lefts = lax.dynamic_slice_in_dim(left_blocks, (left_sector * A).astype(jnp.int32), A, 0).astype(jnp.float32)
        state = lax.dynamic_index_in_dim(wavefunction, index, 0, keepdims=False).astype(jnp.float32)
        lifted = jnp.einsum("aij,jk->aik", lefts, state).astype(jnp.bfloat16)
        row = (source * RUSE + pair_sectors[index, 1]).astype(jnp.int32)
        block_ids = lax.dynamic_index_in_dim(right_env, row, 0, keepdims=False)
        chosen = right_blocks[block_ids].astype(jnp.float32)
        applied = jnp.einsum("aik,amk->aim", lifted.astype(jnp.float32), chosen).astype(jnp.bfloat16)
        weights = channel_mask[index].astype(jnp.float32)
        return jnp.einsum("a,aim->im", weights, applied.astype(jnp.float32))

    return lax.map(one_pair, jnp.arange(NP, dtype=jnp.int32))
```

```python
import functools

import jax
import jax.numpy as jnp
from jax import lax
from jax.experimental import pallas as pl
from jax.experimental.pallas import tpu as pltpu
from jax.sharding import PartitionSpec as P

MESH = pl.DeviceIdType.MESH


def flip(index, step, n):
    out = 0
    bit = 1
    while bit < n:
        out = out + bit * ((index // bit + step // bit) % 2)
        bit *= 2
    return out


def kernel(
    n,
    cap,
    sectors_l,
    channels,
    request_ref,
    entry_ref,
    side_ref,
    place_ref,
    pairs_ref,
    mask_ref,
    psi_ref,
    left_hbm,
    right_hbm,
    out_ref,
    left,
    right,
    asked,
    asked_sc,
    send,
    held,
    lifted,
    total,
    left_sem,
    right_sem,
    ask_send_sem,
    ask_recv_sem,
    table_sem,
    send_sem,
    recv_sem,
):
    me = lax.axis_index("blk")
    tile = psi_ref.shape[1]
    pairs = psi_ref.shape[0]
    right_copy = pltpu.make_async_copy(right_hbm, right, right_sem)
    right_copy.start()

    def left_copy(l):
        return pltpu.make_async_copy(
            left_hbm.at[pl.ds(l * channels, channels)],
            left.at[pl.ds(l * channels, channels)],
            left_sem.at[l],
        )

    for l in range(sectors_l):
        left_copy(l).start()

    barrier = pltpu.get_barrier_semaphore()

    def greet(k, c):
        pl.semaphore_signal(barrier, inc=1, device_id={"blk": flip(me, k, n)}, device_id_type=MESH)
        return c

    lax.fori_loop(1, n, greet, 0)
    pl.semaphore_wait(barrier, n - 1)

    def ask(k):
        peer = flip(me, k, n)
        return pltpu.make_async_remote_copy(
            src_ref=request_ref.at[peer],
            dst_ref=asked.at[k],
            send_sem=ask_send_sem.at[k],
            recv_sem=ask_recv_sem.at[k],
            device_id={"blk": peer},
            device_id_type=MESH,
        )

    def ask_start(k, c):
        ask(n - k).start()
        return c

    lax.fori_loop(1, n, ask_start, 0)
    asked[0] = request_ref[me]

    def reply(k):
        return pltpu.make_async_remote_copy(
            src_ref=send.at[k],
            dst_ref=held.at[k],
            send_sem=send_sem.at[k],
            recv_sem=recv_sem.at[k],
            device_id={"blk": flip(me, k, n)},
            device_id_type=MESH,
        )

    def ask_wait(k, c):
        ask(n - k).wait()
        return c

    lax.fori_loop(1, n, ask_wait, 0)
    table_copy = pltpu.make_async_copy(asked, asked_sc, table_sem)
    table_copy.start()
    right_copy.wait()
    table_copy.wait()

    def pack(i, c):
        k = n - i

        for j in range(cap):
            send[k, j] = right[asked_sc[k, 0, j]]
        reply(k).start()
        return c

    lax.fori_loop(1, n, pack, 0)
    for j in range(cap):
        held[0, j] = right[asked_sc[0, 0, j]]

    def lift(l, c):
        left_copy(l).wait()
        p0 = place_ref[2 * l]
        p1 = place_ref[2 * l + 1]
        state = jnp.concatenate([psi_ref[p0], psi_ref[p1]], axis=1)

        def one(a, c):
            both = jnp.dot(left[l * channels + a], state, preferred_element_type=jnp.float32)
            m0 = mask_ref[p0, a].astype(jnp.float32)
            m1 = mask_ref[p1, a].astype(jnp.float32)
            lifted[a, l] = (both[:, :tile] * m0).astype(jnp.bfloat16)
            lifted[channels + a, l] = (both[:, tile:] * m1).astype(jnp.bfloat16)
            return c

        return lax.fori_loop(0, channels, one, c)

    lax.fori_loop(0, sectors_l, lift, 0)
    total[...] = jnp.zeros_like(total)

    def apply(k):
        peer = flip(me, k, n)

        def two(h, c):
            rows = []
            entries = []
            for j in range(2):
                s = peer * cap + 2 * h + j
                entries.append(entry_ref[s])
                block = held[k, 2 * h + j].astype(jnp.float32)
                w0 = (side_ref[s] % 2).astype(jnp.float32)
                w1 = (side_ref[s] // 2).astype(jnp.float32)
                rows.append(
                    jnp.concatenate([(block * w0).astype(jnp.bfloat16), (block * w1).astype(jnp.bfloat16)], axis=0)
                )
            wide = jnp.concatenate(rows, axis=1)

            for l in range(sectors_l):
                x = jnp.concatenate([lifted[entries[0], l], lifted[entries[1], l]], axis=1)
                total[l] += lax.dot_general(
                    x, wide, (((1,), (1,)), ((), ())), preferred_element_type=jnp.float32
                )
            return c

        lax.fori_loop(0, cap // 2, two, 0)

    apply(0)

    def arrive(i, c):
        k = n - i
        reply(k).wait_recv()
        apply(k)
        return c

    lax.fori_loop(1, n, arrive, 0)

    def finish(p, c):
        both = total[pairs_ref[2 * p]]
        w1 = pairs_ref[2 * p + 1].astype(jnp.float32)
        out_ref[p] = both[:, :tile] * (1.0 - w1) + both[:, tile:] * w1
        return c

    lax.fori_loop(0, pairs, finish, 0)

    def sent(k, c):
        reply(k).wait_send()
        return c

    lax.fori_loop(1, n, sent, 0)


def on_device(n, wavefunction, left_blocks, right_blocks, right_env, pair_sectors, channel_mask):
    pairs, tile = wavefunction.shape[0], wavefunction.shape[1]
    channels = channel_mask.shape[1]
    sides = right_env.shape[0]
    sectors_l = left_blocks.shape[0] // channels
    stored = right_blocks.shape[0]
    used = sides * channels
    cap = max(2, (3 * used + 2 * n - 1) // (2 * n))
    cap += cap % 2

    ids = right_env.reshape(used)
    owners = ids // stored
    order = jnp.arange(used, dtype=jnp.int32)
    same = (owners[:, None] == owners[None, :]) & (order[None, :] < order[:, None])
    rank = jnp.sum(same.astype(jnp.int32), axis=1)
    slot = owners * cap + rank
    chosen = slot[None, :] == jnp.arange(n * cap, dtype=jnp.int32)[:, None]
    entry = jnp.sum(jnp.where(chosen, order[None, :], 0), axis=1)
    side = jnp.sum(jnp.where(chosen, 1 + (order // channels)[None, :], 0), axis=1)
    request = jnp.sum(jnp.where(chosen, (ids % stored)[None, :], 0), axis=1)
    request = jnp.pad(request.reshape(n, 1, cap), ((0, 0), (0, 0), (0, 128 - cap)))
    spot = pair_sectors[:, 0] * sides + pair_sectors[:, 1]
    which = jnp.arange(pairs, dtype=jnp.int32)
    place = jnp.sum(jnp.where(spot[None, :] == which[:, None], which[None, :], 0), axis=1)

    smem = pl.BlockSpec(memory_space=pltpu.SMEM)
    vmem = pl.BlockSpec(memory_space=pltpu.VMEM)
    hbm = pl.BlockSpec(memory_space=pl.ANY)
    return pl.pallas_call(
        functools.partial(kernel, n, cap, sectors_l, channels),
        out_shape=jax.ShapeDtypeStruct((pairs, tile, tile), jnp.float32),
        in_specs=[vmem, smem, smem, smem, smem, smem, vmem, hbm, hbm],
        out_specs=vmem,
        scratch_shapes=[
            pltpu.VMEM(left_blocks.shape, jnp.bfloat16),
            pltpu.VMEM(right_blocks.shape, jnp.bfloat16),
            pltpu.VMEM((n, 1, 128), jnp.int32),
            pltpu.SMEM((n, 1, 128), jnp.int32),
            pltpu.VMEM((n, cap, tile, tile), jnp.bfloat16),
            pltpu.VMEM((n, cap, tile, tile), jnp.bfloat16),
            pltpu.VMEM((used, sectors_l, tile, tile), jnp.bfloat16),
            pltpu.VMEM((sectors_l, tile, 2 * tile), jnp.float32),
            pltpu.SemaphoreType.DMA((sectors_l,)),
            pltpu.SemaphoreType.DMA,
            pltpu.SemaphoreType.DMA((n,)),
            pltpu.SemaphoreType.DMA((n,)),
            pltpu.SemaphoreType.DMA,
            pltpu.SemaphoreType.DMA((n,)),
            pltpu.SemaphoreType.DMA((n,)),
        ],
        compiler_params=pltpu.CompilerParams(
            collective_id=0, has_side_effects=True, vmem_limit_bytes=56 * 1024 * 1024
        ),
    )(
        request,
        entry,
        side,
        place,
        pair_sectors.reshape(-1),
        channel_mask,
        wavefunction,
        left_blocks,
        right_blocks,
    )


def solution(mesh):
    row = P(("groups", "blk"), None)
    block = P(("groups", "blk"), None, None)
    return jax.shard_map(
        functools.partial(on_device, mesh.shape["blk"]),
        mesh=mesh,
        in_specs=(block, block, block, row, row, row),
        out_specs=block,
        check_vma=False,
    )
```

```python
import functools

import jax
import jax.numpy as jnp
from jax import lax
from jax.experimental import pallas as pl
from jax.experimental.pallas import tpu as pltpu
from jax.sharding import PartitionSpec as P

MESH = pl.DeviceIdType.MESH


def flip(index, step, n):
    out = 0
    bit = 1
    while bit < n:
        out = out + bit * ((index // bit + step // bit) % 2)
        bit *= 2
    return out


def kernel(
    n,
    cap,
    env_ref,
    pairs_ref,
    mask_ref,
    psi_ref,
    left_hbm,
    right_hbm,
    out_ref,
    left,
    right,
    table,
    table_sc,
    asked,
    asked_sc,
    send,
    held,
    lifted,
    total,
    left_sem,
    right_sem,
    ask_send_sem,
    ask_recv_sem,
    table_sem,
    send_sem,
    recv_sem,
):
    me = lax.axis_index("blk")
    tile = psi_ref.shape[1]
    pairs = psi_ref.shape[0]
    channels = mask_ref.shape[1]
    sectors_l = total.shape[0]
    stored = right.shape[0]
    lanes = asked.shape[2]

    def step(i):
        return n // 2 + (1 - 2 * (i % 2)) * ((i + 1) // 2)

    right_copy = pltpu.make_async_copy(right_hbm, right, right_sem)
    right_copy.start()

    def left_copy(l):
        return pltpu.make_async_copy(
            left_hbm.at[pl.ds(l * channels, channels)],
            left.at[pl.ds(l * channels, channels)],
            left_sem.at[l],
        )

    for l in range(sectors_l):
        left_copy(l).start()

    barrier = pltpu.get_barrier_semaphore()

    def greet(k, c):
        pl.semaphore_signal(barrier, inc=1, device_id={"blk": flip(me, k, n)}, device_id_type=MESH)
        return c

    lax.fori_loop(1, n, greet, 0)

    used = env_ref.shape[0] * channels
    height = -(-used // 128) * 128
    sides = [env_ref[r : r + 1, :] for r in range(env_ref.shape[0])]
    if height > used:
        sides.append(jnp.full((1, height - used), n * stored, jnp.int32))
    across = jnp.broadcast_to(jnp.concatenate(sides, axis=1), (height, height))
    down = across.T
    first = lax.broadcasted_iota(jnp.int32, (height, height), 0)
    second = lax.broadcasted_iota(jnp.int32, (height, height), 1)
    owner = lax.div(down, jnp.full_like(down, stored))
    same = (owner == lax.div(across, jnp.full_like(across, stored))) & (second < first)
    rank = jnp.sum(same.astype(jnp.int32), axis=1, keepdims=True)
    slot = owner[:, :1] * cap + rank
    entry = lax.broadcasted_iota(jnp.int32, (height, lanes), 0)
    chosen = slot == lax.broadcasted_iota(jnp.int32, (height, lanes), 1)
    local = down[:, :1] - owner[:, :1] * stored

    def picked(values):
        return jnp.sum(jnp.where(chosen, values, 0), axis=0, keepdims=True)

    asked[0] = picked(jnp.broadcast_to(local, (height, lanes)))
    table[0:1, :] = picked(entry)
    table[1:2, :] = picked(1 + (entry >= channels).astype(jnp.int32))
    table_copy = pltpu.make_async_copy(table, table_sc, table_sem.at[0])
    table_copy.start()
    pl.semaphore_wait(barrier, n - 1)

    def ask(k):
        return pltpu.make_async_remote_copy(
            src_ref=asked.at[0],
            dst_ref=asked.at[k],
            send_sem=ask_send_sem.at[k],
            recv_sem=ask_recv_sem.at[k],
            device_id={"blk": flip(me, k, n)},
            device_id_type=MESH,
        )

    def ask_start(i, c):
        ask(step(i)).start()
        return c

    lax.fori_loop(0, n - 1, ask_start, 0)

    def reply(k):
        return pltpu.make_async_remote_copy(
            src_ref=send.at[k],
            dst_ref=held.at[k],
            send_sem=send_sem.at[k],
            recv_sem=recv_sem.at[k],
            device_id={"blk": flip(me, k, n)},
            device_id_type=MESH,
        )

    def ask_wait(i, c):
        ask(step(i)).wait()
        return c

    lax.fori_loop(0, n - 1, ask_wait, 0)
    asked_copy = pltpu.make_async_copy(asked, asked_sc, table_sem.at[1])
    asked_copy.start()
    right_copy.wait()
    asked_copy.wait()

    def pack(i, c):
        k = step(i)
        for j in range(cap):
            send[k, j] = right[asked_sc[k, 0, me * cap + j]]
        reply(k).start()
        return c

    lax.fori_loop(0, n - 1, pack, 0)
    for j in range(cap):
        held[0, j] = right[asked_sc[0, 0, me * cap + j]]

    def lift(l, c):
        left_copy(l).wait()
        p0 = 0
        p1 = 0
        for p in range(pairs):
            spot = 2 * pairs_ref[p, 0] + pairs_ref[p, 1]
            p0 = jnp.where(spot == 2 * l, p, p0)
            p1 = jnp.where(spot == 2 * l + 1, p, p1)
        state = jnp.concatenate([psi_ref[p0], psi_ref[p1]], axis=1)

        def one(a, c):
            both = jnp.dot(left[l * channels + a], state, preferred_element_type=jnp.float32)
            m0 = mask_ref[p0, a].astype(jnp.float32)
            m1 = mask_ref[p1, a].astype(jnp.float32)
            lifted[a, l] = (both[:, :tile] * m0).astype(jnp.bfloat16)
            lifted[channels + a, l] = (both[:, tile:] * m1).astype(jnp.bfloat16)
            return c

        return lax.fori_loop(0, channels, one, c)

    lax.fori_loop(0, sectors_l, lift, 0)
    total[...] = jnp.zeros_like(total)
    table_copy.wait()

    def apply(k):
        peer = flip(me, k, n)

        def two(h, c):
            rows = []
            entries = []
            for j in range(2):
                s = peer * cap + 2 * h + j
                entries.append(table_sc[0, s])
                block = held[k, 2 * h + j].astype(jnp.float32)
                w0 = (table_sc[1, s] % 2).astype(jnp.float32)
                w1 = (table_sc[1, s] // 2).astype(jnp.float32)
                rows.append(
                    jnp.concatenate([(block * w0).astype(jnp.bfloat16), (block * w1).astype(jnp.bfloat16)], axis=0)
                )
            wide = jnp.concatenate(rows, axis=1)

            for l in range(sectors_l):
                x = jnp.concatenate([lifted[entries[0], l], lifted[entries[1], l]], axis=1)
                total[l] += lax.dot_general(
                    x, wide, (((1,), (1,)), ((), ())), preferred_element_type=jnp.float32
                )
            return c

        lax.fori_loop(0, cap // 2, two, 0)

    apply(0)

    def arrive(i, c):
        k = step(i)
        reply(k).wait_recv()
        apply(k)
        return c

    lax.fori_loop(0, n - 1, arrive, 0)

    def finish(p, c):
        both = total[pairs_ref[p, 0]]
        w1 = pairs_ref[p, 1].astype(jnp.float32)
        out_ref[p] = both[:, :tile] * (1.0 - w1) + both[:, tile:] * w1
        return c

    lax.fori_loop(0, pairs, finish, 0)

    def sent(k, c):
        reply(k).wait_send()
        return c

    lax.fori_loop(1, n, sent, 0)


def on_device(n, wavefunction, left_blocks, right_blocks, right_env, pair_sectors, channel_mask):
    pairs, tile = wavefunction.shape[0], wavefunction.shape[1]
    channels = channel_mask.shape[1]
    sides = right_env.shape[0]
    sectors_l = left_blocks.shape[0] // channels
    stored = right_blocks.shape[0]
    used = sides * channels
    cap = max(2, (3 * used + 2 * n - 1) // (2 * n))
    cap += cap % 2

    lanes = -(-n * cap // 128) * 128
    smem = pl.BlockSpec(memory_space=pltpu.SMEM)
    vmem = pl.BlockSpec(memory_space=pltpu.VMEM)
    hbm = pl.BlockSpec(memory_space=pl.ANY)
    return pl.pallas_call(
        functools.partial(kernel, n, cap),
        out_shape=jax.ShapeDtypeStruct((pairs, tile, tile), jnp.float32),
        in_specs=[vmem, smem, smem, vmem, hbm, hbm],
        out_specs=vmem,
        scratch_shapes=[
            pltpu.VMEM(left_blocks.shape, jnp.bfloat16),
            pltpu.VMEM(right_blocks.shape, jnp.bfloat16),
            pltpu.VMEM((2, lanes), jnp.int32),
            pltpu.SMEM((2, lanes), jnp.int32),
            pltpu.VMEM((n, 1, lanes), jnp.int32),
            pltpu.SMEM((n, 1, lanes), jnp.int32),
            pltpu.VMEM((n, cap, tile, tile), jnp.bfloat16),
            pltpu.VMEM((n, cap, tile, tile), jnp.bfloat16),
            pltpu.VMEM((used, sectors_l, tile, tile), jnp.bfloat16),
            pltpu.VMEM((sectors_l, tile, 2 * tile), jnp.float32),
            pltpu.SemaphoreType.DMA((sectors_l,)),
            pltpu.SemaphoreType.DMA,
            pltpu.SemaphoreType.DMA((n,)),
            pltpu.SemaphoreType.DMA((n,)),
            pltpu.SemaphoreType.DMA((2,)),
            pltpu.SemaphoreType.DMA((n,)),
            pltpu.SemaphoreType.DMA((n,)),
        ],
        compiler_params=pltpu.CompilerParams(
            collective_id=0, has_side_effects=True, vmem_limit_bytes=56 * 1024 * 1024
        ),
    )(
        right_env,
        pair_sectors,
        channel_mask,
        wavefunction,
        left_blocks,
        right_blocks,
    )


def solution(mesh):
    row = P(("groups", "blk"), None)
    block = P(("groups", "blk"), None, None)
    return jax.shard_map(
        functools.partial(on_device, mesh.shape["blk"]),
        mesh=mesh,
        in_specs=(block, block, block, row, row, row),
        out_specs=block,
        check_vma=False,
    )
```

```python
import functools

import jax
import jax.numpy as jnp
from jax import lax
from jax.experimental import pallas as pl
from jax.experimental.pallas import tpu as pltpu
from jax.sharding import PartitionSpec as P

MESH = pl.DeviceIdType.MESH


def flip(index, step, n):
    out = 0
    bit = 1
    while bit < n:
        out = out + bit * ((index // bit + step // bit) % 2)
        bit *= 2
    return out


def kernel(
    n,
    cap,
    env_ref,
    pairs_ref,
    mask_ref,
    psi_ref,
    left_hbm,
    right_hbm,
    out_ref,
    left,
    right,
    table,
    table_sc,
    asked,
    asked_sc,
    send,
    held,
    lifted,
    total,
    left_sem,
    right_sem,
    ask_send_sem,
    ask_recv_sem,
    table_sem,
    send_sem,
    recv_sem,
):
    me = lax.axis_index("blk")
    tile = psi_ref.shape[1]
    pairs = psi_ref.shape[0]
    channels = mask_ref.shape[1]
    sectors_l = total.shape[0]
    stored = right.shape[0]
    lanes = asked.shape[2]
    bits = [1 << b for b in range(n.bit_length() - 1)]
    turn = [bit - 2 * bit * ((me // bit) % 2) for bit in bits]

    def partner(k):
        out = me
        for bit, change in zip(bits, turn):
            if k & bit:
                out = out + change
        return out

    def step(i):
        return n // 2 + (1 - 2 * (i % 2)) * ((i + 1) // 2)

    right_copy = pltpu.make_async_copy(right_hbm, right, right_sem)
    right_copy.start()

    def left_copy(l):
        return pltpu.make_async_copy(
            left_hbm.at[pl.ds(l * channels, channels)],
            left.at[pl.ds(l * channels, channels)],
            left_sem.at[l],
        )

    barrier = pltpu.get_barrier_semaphore()

    for i in range(n - 1):
        pl.semaphore_signal(barrier, inc=1, device_id={"blk": partner(step(i))}, device_id_type=MESH)

    used = env_ref.shape[0] * channels
    height = -(-used // 128) * 128
    sides = [env_ref[r : r + 1, :] for r in range(env_ref.shape[0])]
    if height > used:
        sides.append(jnp.full((1, height - used), n * stored, jnp.int32))
    ids = jnp.concatenate(sides, axis=1)
    owners = lax.div(ids, jnp.full_like(ids, stored))
    across = jnp.broadcast_to(owners, (height, height))
    owner = across.T
    local = jnp.broadcast_to(ids - owners * stored, (height, height)).T[:, :1]
    first = lax.broadcasted_iota(jnp.int32, (height, height), 0)
    second = lax.broadcasted_iota(jnp.int32, (height, height), 1)
    same = (owner == across) & (second < first)
    rank = jnp.sum(same.astype(jnp.int32), axis=1, keepdims=True)
    slot = owner[:, :1] * cap + rank
    entry = lax.broadcasted_iota(jnp.int32, (height, lanes), 0)
    chosen = slot == lax.broadcasted_iota(jnp.int32, (height, lanes), 1)

    def picked(values):
        return jnp.sum(jnp.where(chosen, values, 0), axis=0, keepdims=True)

    asked[0] = picked(jnp.broadcast_to(local, (height, lanes)))
    table[0:1, :] = picked(entry)
    table[1:2, :] = picked(1 + (entry >= channels).astype(jnp.int32))
    table_copy = pltpu.make_async_copy(table, table_sc, table_sem.at[0])
    table_copy.start()
    pl.semaphore_wait(barrier, n - 1)

    def ask(k):
        return pltpu.make_async_remote_copy(
            src_ref=asked.at[0],
            dst_ref=asked.at[k],
            send_sem=ask_send_sem.at[k],
            recv_sem=ask_recv_sem.at[k],
            device_id={"blk": partner(k)},
            device_id_type=MESH,
        )

    for i in range(n - 1):
        ask(step(i)).start()

    def reply(k, peer):
        return pltpu.make_async_remote_copy(
            src_ref=send.at[k],
            dst_ref=held.at[k],
            send_sem=send_sem.at[k],
            recv_sem=recv_sem.at[k],
            device_id={"blk": peer},
            device_id_type=MESH,
        )

    early = min(3, n - 1)

    def serve(steps, spans):
        for i in steps:
            ask(step(i)).wait()
        copies = [
            pltpu.make_async_copy(asked.at[pl.ds(a, b - a)], asked_sc.at[pl.ds(a, b - a)], table_sem.at[1 + a])
            for a, b in spans
            if b > a
        ]
        for copy in copies:
            copy.start()
        for copy in copies:
            copy.wait()
        for i in steps:
            k = step(i)
            for j in range(cap):
                send[k, j] = right[asked_sc[k, 0, me * cap + j]]
            reply(k, partner(k)).start()

    low = min(step(i) for i in range(early))
    high = max(step(i) for i in range(early)) + 1
    right_copy.wait()
    serve(range(early), [(low, high)])
    serve(range(early, n - 1), [(0, low), (high, n)])
    for l in range(sectors_l):
        left_copy(l).start()

    for j in range(cap):
        held[0, j] = right[asked_sc[0, 0, me * cap + j]]

    def lift(l, c):
        left_copy(l).wait()
        p0 = 0
        p1 = 0
        for p in range(pairs):
            spot = 2 * pairs_ref[0, p] + pairs_ref[1, p]
            p0 = jnp.where(spot == 2 * l, p, p0)
            p1 = jnp.where(spot == 2 * l + 1, p, p1)
        state = jnp.concatenate([psi_ref[p0], psi_ref[p1]], axis=1)

        def one(a, c):
            both = jnp.dot(left[l * channels + a], state, preferred_element_type=jnp.float32)
            m0 = mask_ref[p0, a].astype(jnp.float32)
            m1 = mask_ref[p1, a].astype(jnp.float32)
            lifted[a, l] = (both[:, :tile] * m0).astype(jnp.bfloat16)
            lifted[channels + a, l] = (both[:, tile:] * m1).astype(jnp.bfloat16)
            return c

        return lax.fori_loop(0, channels, one, c)

    lax.fori_loop(0, sectors_l, lift, 0)
    total[...] = jnp.zeros_like(total)
    table_copy.wait()

    def apply(k):
        peer = flip(me, k, n)

        def two(h, c):
            rows = []
            entries = []
            for j in range(2):
                s = peer * cap + 2 * h + j
                entries.append(table_sc[0, s])
                block = held[k, 2 * h + j].astype(jnp.float32)
                w0 = (table_sc[1, s] % 2).astype(jnp.float32)
                w1 = (table_sc[1, s] // 2).astype(jnp.float32)
                rows.append(
                    jnp.concatenate([(block * w0).astype(jnp.bfloat16), (block * w1).astype(jnp.bfloat16)], axis=0)
                )
            wide = jnp.concatenate(rows, axis=1)

            for l in range(sectors_l):
                x = jnp.concatenate([lifted[entries[0], l], lifted[entries[1], l]], axis=1)
                total[l] += lax.dot_general(
                    x, wide, (((1,), (1,)), ((), ())), preferred_element_type=jnp.float32
                )
            return c

        lax.fori_loop(0, cap // 2, two, 0)

    apply(0)

    def arrive(i, c):
        k = step(i)
        reply(k, flip(me, k, n)).wait_recv()
        apply(k)
        return c

    lax.fori_loop(0, n - 1, arrive, 0)

    def finish(p, c):
        both = total[pairs_ref[0, p]]
        w1 = pairs_ref[1, p].astype(jnp.float32)
        out_ref[p] = both[:, :tile] * (1.0 - w1) + both[:, tile:] * w1
        return c

    lax.fori_loop(0, pairs, finish, 0)

    for k in range(1, n):
        reply(k, partner(k)).wait_send()


def on_device(n, wavefunction, left_blocks, right_blocks, right_env, pair_sectors, channel_mask):
    pairs, tile = wavefunction.shape[0], wavefunction.shape[1]
    channels = channel_mask.shape[1]
    sides = right_env.shape[0]
    sectors_l = left_blocks.shape[0] // channels
    stored = right_blocks.shape[0]
    used = sides * channels
    cap = max(2, (3 * used + 2 * n - 1) // (2 * n))
    cap += cap % 2

    lanes = -(-n * cap // 128) * 128
    smem = pl.BlockSpec(memory_space=pltpu.SMEM)
    vmem = pl.BlockSpec(memory_space=pltpu.VMEM)
    hbm = pl.BlockSpec(memory_space=pl.ANY)
    return pl.pallas_call(
        functools.partial(kernel, n, cap),
        out_shape=jax.ShapeDtypeStruct((pairs, tile, tile), jnp.float32),
        in_specs=[vmem, smem, smem, vmem, hbm, hbm],
        out_specs=vmem,
        scratch_shapes=[
            pltpu.VMEM(left_blocks.shape, jnp.bfloat16),
            pltpu.VMEM(right_blocks.shape, jnp.bfloat16),
            pltpu.VMEM((2, lanes), jnp.int32),
            pltpu.SMEM((2, lanes), jnp.int32),
            pltpu.VMEM((n, 1, lanes), jnp.int32),
            pltpu.SMEM((n, 1, lanes), jnp.int32),
            pltpu.VMEM((n, cap, tile, tile), jnp.bfloat16),
            pltpu.VMEM((n, cap, tile, tile), jnp.bfloat16),
            pltpu.VMEM((used, sectors_l, tile, tile), jnp.bfloat16),
            pltpu.VMEM((sectors_l, tile, 2 * tile), jnp.float32),
            pltpu.SemaphoreType.DMA((sectors_l,)),
            pltpu.SemaphoreType.DMA,
            pltpu.SemaphoreType.DMA((n,)),
            pltpu.SemaphoreType.DMA((n,)),
            pltpu.SemaphoreType.DMA((n + 1,)),
            pltpu.SemaphoreType.DMA((n,)),
            pltpu.SemaphoreType.DMA((n,)),
        ],
        compiler_params=pltpu.CompilerParams(
            collective_id=0, has_side_effects=True, vmem_limit_bytes=56 * 1024 * 1024
        ),
    )(
        right_env,
        pair_sectors.T,
        channel_mask,
        wavefunction,
        left_blocks,
        right_blocks,
    )


def solution(mesh):
    row = P(("groups", "blk"), None)
    block = P(("groups", "blk"), None, None)
    return jax.shard_map(
        functools.partial(on_device, mesh.shape["blk"]),
        mesh=mesh,
        in_specs=(block, block, block, row, row, row),
        out_specs=block,
        check_vma=False,
    )
```

```python
import functools

import jax
import jax.numpy as jnp
from jax import lax
from jax.experimental import pallas as pl
from jax.experimental.pallas import tpu as pltpu
from jax.sharding import PartitionSpec as P

MESH = pl.DeviceIdType.MESH


def flip(index, step, n):
    out = 0
    bit = 1
    while bit < n:
        out = out + bit * ((index // bit + step // bit) % 2)
        bit *= 2
    return out


def kernel(
    n,
    cap,
    env_ref,
    pairs_ref,
    mask_ref,
    psi_ref,
    left_hbm,
    right_hbm,
    out_ref,
    left,
    right,
    table,
    table_sc,
    asked,
    asked_sc,
    send,
    held,
    lifted,
    total,
    left_sem,
    right_sem,
    ask_send_sem,
    ask_recv_sem,
    table_sem,
    send_sem,
    recv_sem,
):
    me = lax.axis_index("blk")
    tile = psi_ref.shape[1]
    pairs = psi_ref.shape[0]
    channels = mask_ref.shape[1]
    sectors_l = total.shape[0]
    stored = right.shape[0]
    lanes = asked.shape[2]
    bits = [1 << b for b in range(n.bit_length() - 1)]
    turn = [bit - 2 * bit * ((me // bit) % 2) for bit in bits]

    def partner(k):
        out = me
        for bit, change in zip(bits, turn):
            if k & bit:
                out = out + change
        return out

    def step(i):
        return n // 2 + (1 - 2 * (i % 2)) * ((i + 1) // 2)

    right_copy = pltpu.make_async_copy(right_hbm, right, right_sem)
    right_copy.start()

    def left_copy(l):
        return pltpu.make_async_copy(
            left_hbm.at[pl.ds(l * channels, channels)],
            left.at[pl.ds(l * channels, channels)],
            left_sem.at[l],
        )

    barrier = pltpu.get_barrier_semaphore()

    for i in range(n - 1):
        pl.semaphore_signal(barrier, inc=1, device_id={"blk": partner(step(i))}, device_id_type=MESH)

    used = env_ref.shape[0] * channels
    height = -(-used // 128) * 128
    sides = [env_ref[r : r + 1, :] for r in range(env_ref.shape[0])]
    if height > used:
        sides.append(jnp.full((1, height - used), n * stored, jnp.int32))
    ids = jnp.concatenate(sides, axis=1)
    owners = lax.div(ids, jnp.full_like(ids, stored))
    across = jnp.broadcast_to(owners, (height, height))
    owner = across.T
    local = jnp.broadcast_to(ids - owners * stored, (height, height)).T[:, :1]
    first = lax.broadcasted_iota(jnp.int32, (height, height), 0)
    second = lax.broadcasted_iota(jnp.int32, (height, height), 1)
    same = (owner == across) & (second < first)
    rank = jnp.sum(same.astype(jnp.int32), axis=1, keepdims=True)
    slot = owner[:, :1] * cap + rank
    entry = lax.broadcasted_iota(jnp.int32, (height, lanes), 0)
    chosen = slot == lax.broadcasted_iota(jnp.int32, (height, lanes), 1)

    def picked(values):
        return jnp.sum(jnp.where(chosen, values, 0), axis=0, keepdims=True)

    asked[0] = picked(jnp.broadcast_to(local, (height, lanes)))
    table[0:1, :] = picked(entry)
    table[1:2, :] = picked(1 + (entry >= channels).astype(jnp.int32))
    table_copy = pltpu.make_async_copy(table, table_sc, table_sem.at[0])
    table_copy.start()
    pl.semaphore_wait(barrier, n - 1)

    def ask(k):
        return pltpu.make_async_remote_copy(
            src_ref=asked.at[0],
            dst_ref=asked.at[k],
            send_sem=ask_send_sem.at[k],
            recv_sem=ask_recv_sem.at[k],
            device_id={"blk": partner(k)},
            device_id_type=MESH,
        )

    for i in range(n - 1):
        ask(step(i)).start()

    def reply(k, peer):
        return pltpu.make_async_remote_copy(
            src_ref=send.at[k],
            dst_ref=held.at[k],
            send_sem=send_sem.at[k],
            recv_sem=recv_sem.at[k],
            device_id={"blk": peer},
            device_id_type=MESH,
        )

    early = min(3, n - 1)

    def serve(steps, spans):
        for i in steps:
            ask(step(i)).wait()
        copies = [
            pltpu.make_async_copy(asked.at[pl.ds(a, b - a)], asked_sc.at[pl.ds(a, b - a)], table_sem.at[1 + a])
            for a, b in spans
            if b > a
        ]
        for copy in copies:
            copy.start()
        for copy in copies:
            copy.wait()
        for i in steps:
            k = step(i)
            for j in range(cap):
                send[k, j] = right[asked_sc[k, 0, me * cap + j]]
            reply(k, partner(k)).start()

    low = min(step(i) for i in range(early))
    high = max(step(i) for i in range(early)) + 1
    right_copy.wait()
    serve(range(early), [(low, high)])
    serve(range(early, n - 1), [(0, low), (high, n)])
    for l in range(sectors_l):
        left_copy(l).start()

    for j in range(cap):
        held[0, j] = right[asked_sc[0, 0, me * cap + j]]

    def lift(l, c):
        left_copy(l).wait()
        p0 = 0
        p1 = 0
        for p in range(pairs):
            spot = 2 * pairs_ref[0, p] + pairs_ref[1, p]
            p0 = jnp.where(spot == 2 * l, p, p0)
            p1 = jnp.where(spot == 2 * l + 1, p, p1)
        state = jnp.concatenate([psi_ref[p0], psi_ref[p1]], axis=1)

        def one(a, c):
            both = jnp.dot(left[l * channels + a], state, preferred_element_type=jnp.float32)
            m0 = mask_ref[p0, a].astype(jnp.float32)
            m1 = mask_ref[p1, a].astype(jnp.float32)
            lifted[a, l] = (both[:, :tile] * m0).astype(jnp.bfloat16)
            lifted[channels + a, l] = (both[:, tile:] * m1).astype(jnp.bfloat16)
            return c

        return lax.fori_loop(0, channels, one, c)

    lax.fori_loop(0, sectors_l, lift, 0)
    total[...] = jnp.zeros_like(total)
    table_copy.wait()

    def apply(k):
        peer = flip(me, k, n)

        def two(h, c):
            rows = []
            entries = []
            for j in range(2):
                s = peer * cap + 2 * h + j
                entries.append(table_sc[0, s])
                block = held[k, 2 * h + j].astype(jnp.float32)
                w0 = (table_sc[1, s] % 2).astype(jnp.float32)
                w1 = (table_sc[1, s] // 2).astype(jnp.float32)
                rows.append(
                    jnp.concatenate([(block * w0).astype(jnp.bfloat16), (block * w1).astype(jnp.bfloat16)], axis=0)
                )
            wide = jnp.concatenate(rows, axis=1)

            for l in range(sectors_l):
                x = jnp.concatenate([lifted[entries[0], l], lifted[entries[1], l]], axis=1)
                total[l] += lax.dot_general(
                    x, wide, (((1,), (1,)), ((), ())), preferred_element_type=jnp.float32
                )
            return c

        lax.fori_loop(0, cap // 2, two, 0)

    apply(0)

    def arrive(i, c):
        k = step(i)
        reply(k, flip(me, k, n)).wait_recv()
        apply(k)
        return c

    lax.fori_loop(0, n - 1, arrive, 0)

    def finish(p, c):
        both = total[pairs_ref[0, p]]
        w1 = pairs_ref[1, p].astype(jnp.float32)
        out_ref[p] = both[:, :tile] * (1.0 - w1) + both[:, tile:] * w1
        return c

    lax.fori_loop(0, pairs, finish, 0)

    for k in range(1, n):
        reply(k, partner(k)).wait_send()


def on_device(n, wavefunction, left_blocks, right_blocks, right_env, pair_sectors, channel_mask):
    pairs, tile = wavefunction.shape[0], wavefunction.shape[1]
    channels = channel_mask.shape[1]
    sides = right_env.shape[0]
    sectors_l = left_blocks.shape[0] // channels
    stored = right_blocks.shape[0]
    used = sides * channels
    cap = max(2, (3 * used + 2 * n - 1) // (2 * n))
    cap += cap % 2

    lanes = -(-n * cap // 128) * 128
    smem = pl.BlockSpec(memory_space=pltpu.SMEM)
    vmem = pl.BlockSpec(memory_space=pltpu.VMEM)
    hbm = pl.BlockSpec(memory_space=pl.ANY)
    return pl.pallas_call(
        functools.partial(kernel, n, cap),
        out_shape=pltpu.VMEM((pairs, tile, tile), jnp.float32),
        in_specs=[vmem, smem, smem, vmem, hbm, hbm],
        out_specs=vmem,
        scratch_shapes=[
            pltpu.VMEM(left_blocks.shape, jnp.bfloat16),
            pltpu.VMEM(right_blocks.shape, jnp.bfloat16),
            pltpu.VMEM((2, lanes), jnp.int32),
            pltpu.SMEM((2, lanes), jnp.int32),
            pltpu.VMEM((n, 1, lanes), jnp.int32),
            pltpu.SMEM((n, 1, lanes), jnp.int32),
            pltpu.VMEM((n, cap, tile, tile), jnp.bfloat16),
            pltpu.VMEM((n, cap, tile, tile), jnp.bfloat16),
            pltpu.VMEM((used, sectors_l, tile, tile), jnp.bfloat16),
            pltpu.VMEM((sectors_l, tile, 2 * tile), jnp.float32),
            pltpu.SemaphoreType.DMA((sectors_l,)),
            pltpu.SemaphoreType.DMA,
            pltpu.SemaphoreType.DMA((n,)),
            pltpu.SemaphoreType.DMA((n,)),
            pltpu.SemaphoreType.DMA((n + 1,)),
            pltpu.SemaphoreType.DMA((n,)),
            pltpu.SemaphoreType.DMA((n,)),
        ],
        compiler_params=pltpu.CompilerParams(
            collective_id=0, has_side_effects=True, vmem_limit_bytes=56 * 1024 * 1024
        ),
    )(
        right_env,
        pair_sectors.T,
        channel_mask,
        wavefunction,
        left_blocks,
        right_blocks,
    )


def solution(mesh):
    row = P(("groups", "blk"), None)
    block = P(("groups", "blk"), None, None)
    return jax.shard_map(
        functools.partial(on_device, mesh.shape["blk"]),
        mesh=mesh,
        in_specs=(block, block, block, row, row, row),
        out_specs=block,
        check_vma=False,
    )
```
